512 devices in a mesh: branch: 8 (over z_lo), shard: 64 (over x, y, z_hi, core).
Axes of the slice: x: 4, y: 4, z: 16 (z_hi: 2, z_lo: 8; z = z_hi * 8 + z_lo), core: 2. Of those that a mesh axis runs over, the one named last changes fastest.
Arguments:
- key_weights: bfloat16 [8, 8192, 512], P('branch', 'shard'), may hold values from -3 to 3
- first_moment: float32 [8, 8192, 512], P('branch', 'shard'), may hold values from -6 to 6
- second_moment: float32 [8, 8192, 512], P('branch', 'shard'), may hold values from 0.01 to 4
- tokens: bfloat16 [1024, 8192], P('branch', 'shard'), may hold values from -6 to 6
- routes: int32 [1024, 2], P('branch'), may hold values from 0 to 7, all different within a row; in each aligned block of 128 rows (0 to 127, 128 to 255, ...) at most 64 rows name the same one
- route_weights: float32 [1024, 2], P('branch'), may hold values from 0.2 to 1
- gate_up: bfloat16 [8, 2, 4096, 8192], P('branch', None, 'shard'), may hold values from -0.0625 to 0.0625
- down_proj: bfloat16 [8, 4096, 8192], P('branch', None, 'shard'), may hold values from -0.09375 to 0.09375
Outputs:
- merged_key: bfloat16 [8192, 512], P('shard')
- merged_first: float32 [8192, 512], P('shard')
- merged_second: float32 [8192, 512], P('shard')
- mixed: bfloat16 [1024, 8192], P('branch', 'shard')
The draws below stay inside these ranges and needn't reach their ends.
Inputs may be any that keep to these rules, and one draw needn't show every extreme that they name: `routes`: the two experts of a token differ. Among the 128 tokens of one branch group no expert is named by more than 64 tokens, a bound that some block reaches.
All inputs are finite; a program needn't handle non-finite values.
Results may differ from the reference program's by a relative error of at most 0.0058.
Values may be sent and summed in bfloat16 or wider, within the bound.
No kernel may reach another device: no remote copies, remote signals or barrier semaphores. Data moves between devices by JAX's collectives and lax.ppermute only.
A program may use at most 64 MiB of HBM per device.

```python
import math
import jax
import jax.numpy as jnp
import numpy as np
from jax import lax

D = 8192
KW = 512
FF = 4096
TOK_BR = 128
EXPERTS = 8
CAP = 64
TOKENS = 1024
N_BRANCH = 8


def levels(key, extent, pieces, least, high):
    def one(dim, blocks):
        heights = jax.random.uniform(jax.random.fold_in(jax.random.fold_in(key, 6), dim), (blocks,), jnp.float32, least / len(pieces), high / len(pieces))
        return jnp.repeat(jnp.exp(heights), extent[dim] // blocks).reshape((-1,) + (1,) * (len(extent) - dim - 1))

    loudness = one(*pieces[0])
    for cut in pieces[1:]:
        loudness = loudness * one(*cut)
    return loudness


def assign_block(own_key, own, number, rows, number_of, top, limit, lean):
    order = jax.random.permutation(own_key, number_of)
    packed, usual = portions_of(number_of, rows * top, limit, lean, True), portions_of(number_of, rows * top, limit, lean, False)
    places = jnp.arange(number_of)

    def named(lengths, rotation):
        used = int((lengths > 0).sum())
        fixed = max(1, used // 4)
        shifted = fixed + (places - fixed + rotation * (used - fixed)) % max(1, number_of - fixed)
        return jnp.zeros((number_of,), jnp.int32).at[order[jnp.where(places < fixed, places, shifted)]].set(jnp.asarray(lengths, jnp.int32))

    lengths = jnp.where(number % 4 == 0, named(packed, number // 4), named(usual, number - number // 4 - 1))
    mixed = jax.random.permutation(jax.random.fold_in(own, 3), number_of)
    giver, receiver = mixed[0:number_of // 2 * 2:2], mixed[1:number_of // 2 * 2:2]
    slack = jnp.minimum(lengths[giver] - 1, limit - lengths[receiver]) // 2
    slack = jnp.where((giver == order[0]) | (receiver == order[0]) | (lengths[receiver] == 0), 0, jnp.maximum(slack, 0))
    shifted = jax.random.randint(jax.random.fold_in(own, 4), (number_of // 2,), 0, 1 << 20) % (slack + 1)
    lengths = lengths.at[giver].add(-shifted).at[receiver].add(shifted)
    items = jnp.searchsorted(jnp.cumsum(lengths), jnp.arange(rows * top), side="right").astype(jnp.int32)
    listing = items.reshape(top, rows).T
    listing = listing[jax.random.permutation(jax.random.fold_in(own, 1), rows)]
    rotation = jax.random.randint(jax.random.fold_in(own, 2), (rows, 1), 0, top)
    return jnp.take_along_axis(listing, (jnp.arange(top)[None, :] + rotation) % top, axis=1)


def portions_of(amount, total, reach, lean, full):
    loads = [(1 << 20) // math.isqrt(standing ** lean) + 1 for standing in range(1, amount + 1)]
    largest = reach if full else min(reach, max(-(-total // amount), total * loads[0] // sum(loads)))
    least = 1 if total - largest >= amount - 1 else 0
    holding, surplus = [largest] + [least] * (amount - 1), total - largest - least * (amount - 1)
    while surplus > 0:
        free = [i for i in range(1, amount) if holding[i] < largest] or [i for i in range(1, amount) if holding[i] < reach]
        whole, remaining = sum([loads[i] for i in free]), surplus
        for i in free:
            addition = min(reach - holding[i], max(1, remaining * loads[i] // whole), surplus)
            holding[i] = holding[i] + addition
            surplus = surplus - addition
    return np.array(holding)


def centred(rng, dims, deviation, most, cuts=(), kind=jnp.bfloat16):
    result = jax.random.normal(rng, dims, jnp.float32) * deviation
    if len(cuts) > 0:
        result = levels(rng, dims, cuts, -0.22, 0.18) * result
    return jnp.clip(result, min=-most, max=most).astype(kind)


def setup_inputs(seed: int = 0) -> dict:
    arg_keys = jax.random.split(jax.random.key(seed), 9)
    key_weights = centred(arg_keys[0], (EXPERTS, D, KW), 0.5, 3.0, ((0, 8), (1, 64)))
    first_moment = centred(arg_keys[1], (EXPERTS, D, KW), 1.0, 6.0, ((0, 8), (1, 64)), jnp.float32)
    second_moment = jnp.clip(jnp.exp(math.log(4.0) - 5.9914646 * jax.random.uniform(arg_keys[2], (EXPERTS, D, KW), jnp.float32) ** levels(arg_keys[2], (EXPERTS, D, KW), ((0, 8), (1, 64)), -0.2, 0.2)), 0.01, 4.0)
    tokens = centred(arg_keys[3], (TOKENS, D), 1.0, 6.0, ((0, 8), (1, 64)))
    routes_keys = jax.random.split(jax.random.fold_in(arg_keys[4], 1), TOKENS // TOK_BR)
    routes_turns = jax.random.permutation(jax.random.fold_in(arg_keys[4], 3), TOKENS // TOK_BR)
    routes = jax.vmap(lambda own, number: assign_block(jax.random.fold_in(arg_keys[4], 2), own, number, TOK_BR, EXPERTS, 2, CAP, 2))(routes_keys, routes_turns).reshape((TOKENS, 2))
    route_weights = jnp.clip(0.2 + 0.8 * jax.random.uniform(arg_keys[5], (TOKENS, 2), jnp.float32) ** levels(arg_keys[5], (TOKENS, 2), ((0, 8),), -0.2, 0.2), 0.2, 1.0)
    gate_up = centred(arg_keys[6], (EXPERTS, 2, FF, D), D ** -0.5, 0.0625, ((0, 8), (2, 64)))
    down_proj = centred(arg_keys[7], (EXPERTS, FF, D), FF ** -0.5, 0.09375, ((0, 8), (2, 64)))
    return {"key_weights": key_weights, "first_moment": first_moment, "second_moment": second_moment, "tokens": tokens, "routes": routes, "route_weights": route_weights, "gate_up": gate_up, "down_proj": down_proj}


def reference(key_weights, first_moment, second_moment, tokens, routes, route_weights, gate_up, down_proj):
    merged_key = (jnp.sum(key_weights.astype(jnp.float32), axis=0) / N_BRANCH).astype(jnp.bfloat16)
    merged_first = jnp.sum(first_moment, axis=0) / N_BRANCH
    merged_second = jnp.sum(second_moment, axis=0) / N_BRANCH
    grouped = routes.reshape(N_BRANCH, TOK_BR, 2).astype(jnp.int32)
    labels = jnp.arange(EXPERTS, dtype=jnp.int32)
    onehot = (grouped[..., None] == labels).astype(jnp.int32)
    named = jnp.sum(onehot, axis=2)
    before = jnp.cumsum(named, axis=1) - named
    position = jnp.sum(onehot * before[:, :, None, :], axis=-1)
    slot = (grouped * CAP + position).astype(jnp.int32)
    source = jnp.broadcast_to(jnp.arange(N_BRANCH, dtype=jnp.int32)[:, None, None], slot.shape)
    rows_all = tokens.reshape(N_BRANCH, TOK_BR, D)
    payload = jnp.broadcast_to(rows_all[:, :, None, :], (N_BRANCH, TOK_BR, 2, D))
    buffer = jnp.zeros((N_BRANCH, EXPERTS * CAP, D), jnp.bfloat16).at[source, slot].set(payload)
    per_expert = buffer.reshape(N_BRANCH, EXPERTS, CAP, D).transpose(1, 0, 2, 3).reshape(EXPERTS, N_BRANCH * CAP, D)

    def expert_block(items):
        inputs, weights, lower = items
        gate = jnp.dot(inputs, weights[0].T, preferred_element_type=jnp.float32)
        upper = jnp.dot(inputs, weights[1].T, preferred_element_type=jnp.float32)
        hidden = (jax.nn.silu(gate) * upper).astype(jnp.bfloat16)
        return jnp.dot(hidden, lower, preferred_element_type=jnp.float32).astype(jnp.bfloat16)

    outputs = lax.map(expert_block, (per_expert, gate_up, down_proj))
    back = outputs.reshape(EXPERTS, N_BRANCH, CAP, D).transpose(1, 0, 2, 3).reshape(N_BRANCH, EXPERTS * CAP, D)
    picked = back[source, slot].astype(jnp.float32)
    scales = route_weights.reshape(N_BRANCH, TOK_BR, 2)
    mixed = scales[..., 0:1] * picked[:, :, 0] + scales[..., 1:2] * picked[:, :, 1]
    return merged_key, merged_first, merged_second, mixed.reshape(TOKENS, D).astype(jnp.bfloat16)
```

```python
import jax
import jax.numpy as jnp
from jax import lax
from jax.experimental import pallas as pl
from jax.experimental.pallas import tpu as pltpu
from jax.sharding import Mesh
from jax.sharding import PartitionSpec as P

SIDE = 4
GATE_ORDER, DOWN_ORDER = (0, 1, 3, 2), (0, 2, 1, 3)
VMEM = 48 * 1024 * 1024
BF16, F32 = jnp.bfloat16, jnp.float32
SHARD = ("x", "y", "zh", "c")


def shift(array, axis, step):
    size = lax.axis_size(axis)
    return lax.ppermute(array, axis, [(i, (i + step) % size) for i in range(size)])


def flip(array, axis, bit=1):
    return lax.ppermute(array, axis, [(i, i ^ bit) for i in range(lax.axis_size(axis))])


def exchange(blocks, axis):
    return lax.all_to_all(blocks, axis, split_axis=0, concat_axis=0, tiled=True)


def gather(block, axis):
    size = lax.axis_size(axis)
    return exchange(jnp.broadcast_to(block[None], (size,) + block.shape), axis)


def to_peers(cuts, order):
    return [shift(cuts[step], "x", step) if step else cuts[step] for step in order]


def call(kernel, out_shape, at, *arrays):
    many = isinstance(out_shape, (list, tuple))
    vmem = pl.BlockSpec(memory_space=pltpu.VMEM)
    return pl.pallas_call(
        kernel,
        out_shape=out_shape,
        in_specs=[pl.BlockSpec(memory_space=pltpu.SMEM)] + [vmem] * len(arrays),
        out_specs=[vmem] * len(out_shape) if many else vmem,
        compiler_params=pltpu.CompilerParams(vmem_limit_bytes=VMEM),
    )(at, *arrays)


def route_kernel(at_ref, routes_ref, tokens_ref, slotted_ref, pick_ref):
    rows = tokens_ref.shape[0]
    slots = slotted_ref.shape[0] // 2
    experts = 8
    capacity = slots // experts
    label = lax.broadcasted_iota(jnp.int32, (experts, rows), 0)
    first = (routes_ref[0:1, :] == label).astype(F32)
    second = (routes_ref[1:2, :] == label).astype(F32)
    named = first + second
    earlier = (
        lax.broadcasted_iota(jnp.int32, (rows, rows), 0)
        < lax.broadcasted_iota(jnp.int32, (rows, rows), 1)
    ).astype(F32)
    before = jnp.dot(named, earlier, preferred_element_type=F32).astype(jnp.int32)
    position = lax.broadcasted_iota(jnp.int32, (capacity, rows), 0)
    members = []
    for e in range(experts):
        hit = (before[e : e + 1] == position).astype(F32)
        span = slice(e * capacity, (e + 1) * capacity)
        pick_ref[span, :rows] = (hit * first[e : e + 1]).astype(BF16)
        pick_ref[span, rows:] = (hit * second[e : e + 1]).astype(BF16)
        members.append((hit * named[e : e + 1]).astype(BF16))
    slotted = jnp.dot(
        jnp.concatenate(members, axis=0), tokens_ref[...], preferred_element_type=F32
    ).astype(BF16)
    slotted_ref[:slots] = slotted
    slotted_ref[slots:] = slotted


def split_kernel(at_ref, gate_ref, *out_refs):
    wide, cols = gate_ref.shape[1] // SIDE, gate_ref.shape[0]
    for step, out_ref in enumerate(out_refs):
        x = lax.rem(at_ref[0] + step, SIDE)
        for j in range(wide // 128):
            lanes = pl.ds(pl.multiple_of(x * wide + j * 128, 128), 128)
            out_ref[j * cols : (j + 1) * cols, :] = gate_ref[:, lanes]


def gate_kernel(at_ref, w0, w1, w2, w3, own_ref, other_ref, here_ref, out_ref):
    rows = jnp.concatenate(
        [ref[y] for ref in (own_ref, other_ref) for y in range(SIDE)], axis=1
    )
    for step, w_ref in zip(GATE_ORDER, (w0, w1, w2, w3)):
        x = lax.rem(at_ref[0] + SIDE - step, SIDE)
        parts = []
        for core in (at_ref[2], 1 - at_ref[2]):
            for ahead in range(SIDE):
                chip = lax.rem(at_ref[1] + ahead, SIDE) * 2
                for half in range(2):
                    j = (chip + half) * 2 + core
                    parts.append(w_ref[pl.ds(pl.multiple_of(j * 128, 128), 128), :])
        total = lax.dot_general(
            jnp.concatenate(parts, axis=1),
            rows,
            (((1,), (1,)), ((), ())),
            preferred_element_type=F32,
        )
        out_ref[x] = total.astype(BF16)
        if step == 0:
            here_ref[...] = total


def down_kernel(at_ref, w0, w1, w2, w3, own_ref, other_ref, here_ref, out_ref):
    hidden = jnp.concatenate(
        [ref[y] for ref in (own_ref, other_ref) for y in range(SIDE)], axis=0
    )
    deep = own_ref.shape[1] // 2
    for step, w_ref in zip(DOWN_ORDER, (w0, w1, w2, w3)):
        x = lax.rem(at_ref[0] + SIDE - step, SIDE)
        parts = [
            w_ref[pl.ds(pl.multiple_of((chip * 2 + core) * deep, deep), deep), :]
            for core in (at_ref[2], 1 - at_ref[2])
            for chip in range(2 * SIDE)
        ]
        total = lax.dot_general(
            hidden,
            jnp.concatenate(parts, axis=0),
            (((0,), (0,)), ((), ())),
            preferred_element_type=F32,
        )
        out_ref[x] = total.astype(BF16)
        if step == 0:
            here_ref[...] = total


def partial_sums(kernel, shape, at, *arrays):
    shapes = [jax.ShapeDtypeStruct(shape, F32), jax.ShapeDtypeStruct((SIDE,) + shape, BF16)]
    return call(kernel, shapes, at, *arrays)


def add_back(here, got, x):
    for step in range(SIDE):
        here = here + jnp.where(x == step, 0.0, got[step].astype(F32))
    return here


def body(
    key_weights, first_moment, second_moment, tokens, routes, route_weights, gate_up, down_proj
):
    branches = lax.axis_size("b")
    half, x = lax.axis_index("zh"), lax.axis_index("x")
    at = jnp.stack([x, lax.axis_index("y"), lax.axis_index("c")]).astype(jnp.int32)
    branch = lax.axis_index("b")
    group_rows, width = tokens.shape
    capacity = 4 * group_rows // branches
    slots = branches * capacity
    hidden_here = gate_up.shape[2]
    rows_here = key_weights.shape[1]

    slotted, pick = call(
        route_kernel,
        [
            jax.ShapeDtypeStruct((2 * slots, width), BF16),
            jax.ShapeDtypeStruct((slots, 2 * group_rows), BF16),
        ],
        at,
        routes.T,
        tokens,
    )
    arrived = exchange(slotted.reshape(2 * branches, capacity, width), ("zh", "b"))

    gate_w = gate_up[0].reshape(2 * hidden_here, -1)
    cuts = call(
        split_kernel,
        [jax.ShapeDtypeStruct((gate_w.size // SIDE // width, width), BF16)] * SIDE,
        at,
        gate_w,
    )

    slabs = jnp.concatenate(
        [key_weights[0], first_moment[0].astype(BF16), second_moment[0].astype(BF16)], axis=0
    )
    slabs = slabs.reshape(2, 2, -1, slabs.shape[1])
    low, mid = branch % 2, (branch // 2) % 2
    give = lax.dynamic_index_in_dim(slabs, 1 - low, 0, keepdims=False)
    keep = lax.dynamic_index_in_dim(slabs, low, 0, keepdims=False)
    cuts, give = lax.optimization_barrier((cuts, give))
    weights = to_peers(cuts, GATE_ORDER)
    got = flip(give, "b", 1)
    arrived, got = lax.optimization_barrier((arrived, got))

    arrived = arrived.reshape(2, slots, width)
    rows = jnp.concatenate([arrived[0], arrived[1]], axis=1)
    line = [rows] + [shift(rows, "y", -ahead) for ahead in (1, 2, 3)]
    line, weights = lax.optimization_barrier((line, weights))
    line = jnp.stack(line)
    line_other = flip(line, "c")

    slabs = keep.astype(F32) + got.astype(F32)
    give = lax.dynamic_index_in_dim(slabs, 1 - mid, 0, keepdims=False).astype(BF16)
    keep = lax.dynamic_index_in_dim(slabs, mid, 0, keepdims=False)
    got = flip(give, "b", 2)

    here, others = partial_sums(
        gate_kernel,
        (2 * hidden_here, slots),
        at,
        *weights,
        line,
        line_other,
    )
    others, got = lax.optimization_barrier((others, got))
    slabs = (keep.astype(BF16).astype(F32) + got.astype(F32)).astype(BF16)
    got = flip(slabs, "b", 4)
    gated = add_back(here, exchange(others, "x"), x)
    hidden = (jax.nn.silu(gated[:hidden_here]) * gated[hidden_here:]).astype(BF16)

    swap = flip(hidden, "zh")
    lower = down_proj[0].reshape(SIDE, -1, width)
    cuts = [lower[lax.rem(x + step, SIDE)] for step in range(SIDE)]
    cuts, hidden = lax.optimization_barrier((cuts, hidden))
    weights = to_peers(cuts, DOWN_ORDER)
    swap, got = lax.optimization_barrier((swap, got))
    slabs = ((slabs.astype(F32) + got.astype(F32)) / branches).astype(BF16)
    got = flip(slabs, "b", 2)
    both = jnp.where(
        half == 0,
        jnp.concatenate([hidden, swap], axis=0),
        jnp.concatenate([swap, hidden], axis=0),
    )
    line = gather(both, "y")
    line, weights, got = lax.optimization_barrier((line, weights, got))
    slabs = jnp.stack([jnp.where(mid == 0, slabs, got), jnp.where(mid == 0, got, slabs)])
    got = flip(slabs, "b", 1)
    here, others = partial_sums(
        down_kernel, (slots, width), at, *weights, line, flip(line, "c")
    )
    others, got = lax.optimization_barrier((others, got))
    out = add_back(here, exchange(others, "x"), x).astype(BF16)
    out, slabs, got = lax.optimization_barrier((out, slabs, got))

    back = exchange(out.reshape(branches, capacity, width), "b").reshape(slots, width)
    slabs = jnp.stack([jnp.where(low == 0, slabs, got), jnp.where(low == 0, got, slabs)])
    slabs = slabs.reshape(3 * rows_here, -1)
    picked = lax.dot_general(
        pick, back, (((0,), (0,)), ((), ())), preferred_element_type=F32
    )
    mixed = (
        route_weights[:, 0:1] * picked[:group_rows] + route_weights[:, 1:2] * picked[group_rows:]
    ).astype(BF16)
    return (
        slabs[:rows_here],
        slabs[rows_here : 2 * rows_here].astype(F32),
        slabs[2 * rows_here :].astype(F32),
        mixed,
    )


def solution(mesh):
    fine = Mesh(mesh.devices.reshape(8, SIDE, SIDE, 2, 2), ("b",) + SHARD)
    return jax.shard_map(
        body,
        mesh=fine,
        in_specs=(
            P("b", SHARD, None),
            P("b", SHARD, None),
            P("b", SHARD, None),
            P("b", SHARD),
            P("b", None),
            P("b", None),
            P("b", None, SHARD, None),
            P("b", None, SHARD),
        ),
        out_specs=(P(SHARD, None), P(SHARD, None), P(SHARD, None), P("b", SHARD)),
        check_vma=False,
    )
```

```python
import jax
import jax.numpy as jnp
from jax import lax
from jax.experimental import pallas as pl
from jax.experimental.pallas import tpu as pltpu
from jax.sharding import Mesh
from jax.sharding import PartitionSpec as P

SIDE = 4
GATE_ORDER = (0, 1, 3, 2)
ROWS_ORDER = (0, 1, 2, 3)
VMEM = 24 * 1024 * 1024
BF16, F32 = jnp.bfloat16, jnp.float32
SHARD = ("x", "y", "zh", "c")


def shift(array, axis, step):
    size = lax.axis_size(axis)
    return lax.ppermute(array, axis, [(i, (i + step) % size) for i in range(size)])


def flip(array, axis, bit=1):
    return lax.ppermute(array, axis, [(i, i ^ bit) for i in range(lax.axis_size(axis))])


def exchange(blocks, axis):
    return lax.all_to_all(blocks, axis, split_axis=0, concat_axis=0, tiled=True)


def gather(block, axis):
    size = lax.axis_size(axis)
    return exchange(jnp.broadcast_to(block[None], (size,) + block.shape), axis)


def to_peers(cuts, order):
    return [shift(cuts[step], "x", step) if step else cuts[step] for step in order]


def in_hbm(array):
    return pltpu.with_memory_space_constraint(array, pltpu.HBM)


def call(kernel, out_shape, at, *arrays, spaces=None, out_spaces=None, scratch=()):
    spaces = spaces or [pltpu.VMEM] * len(arrays)
    out_spaces = out_spaces or [pltpu.VMEM] * len(out_shape)
    return pl.pallas_call(
        kernel,
        out_shape=out_shape,
        in_specs=[pl.BlockSpec(memory_space=space) for space in [pltpu.SMEM] + list(spaces)],
        out_specs=[pl.BlockSpec(memory_space=space) for space in out_spaces],
        scratch_shapes=list(scratch),
        compiler_params=pltpu.CompilerParams(vmem_limit_bytes=VMEM),
    )(at, *arrays)


def route_kernel(
    at_ref, routes_hbm, tokens_hbm, slotted_ref, pick_ref, routes_ref, tokens_ref, sems
):
    reads = [
        pltpu.make_async_copy(routes_hbm, routes_ref, sems.at[0]),
        pltpu.make_async_copy(tokens_hbm, tokens_ref, sems.at[1]),
    ]
    for read in reads:
        read.start()
    for read in reads:
        read.wait()
    rows = tokens_ref.shape[0]
    slots = slotted_ref.shape[0] // 2
    experts = 8
    capacity = slots // experts
    label = lax.broadcasted_iota(jnp.int32, (experts, rows), 0)
    first = (routes_ref[0:1, :] == label).astype(F32)
    second = (routes_ref[1:2, :] == label).astype(F32)
    named = first + second
    earlier = (
        lax.broadcasted_iota(jnp.int32, (rows, rows), 0)
        < lax.broadcasted_iota(jnp.int32, (rows, rows), 1)
    ).astype(F32)
    before = jnp.dot(named, earlier, preferred_element_type=F32).astype(jnp.int32)
    position = lax.broadcasted_iota(jnp.int32, (capacity, rows), 0)
    members = []
    for e in range(experts):
        hit = (before[e : e + 1] == position).astype(F32)
        span = slice(e * capacity, (e + 1) * capacity)
        pick_ref[span, :rows] = (hit * first[e : e + 1]).astype(BF16)
        pick_ref[span, rows:] = (hit * second[e : e + 1]).astype(BF16)
        members.append((hit * named[e : e + 1]).astype(BF16))
    slotted = jnp.dot(
        jnp.concatenate(members, axis=0), tokens_ref[...], preferred_element_type=F32
    ).astype(BF16)
    slotted_ref[:slots] = slotted
    slotted_ref[slots:] = slotted


def split_kernel(
    at_ref, gate_ref, key_hbm, first_hbm, second_hbm, down_hbm,
    c0, c1, c2, c3, keep_ref, give_ref, lower_ref, key_ref, first_ref, second_ref, sems,
):
    copies = [
        pltpu.make_async_copy(source, target, sems.at[i])
        for i, (source, target) in enumerate(
            (
                (key_hbm, key_ref),
                (first_hbm, first_ref),
                (second_hbm, second_ref),
                (down_hbm.at[:, 1 - at_ref[2]], lower_ref),
            )
        )
    ]
    for copy in copies:
        copy.start()
    wide, cols = gate_ref.shape[1] // SIDE, gate_ref.shape[0]
    for step, out_ref in enumerate((c0, c1, c2, c3)):
        x = lax.rem(at_ref[0] + step, SIDE)
        for j in range(wide // 128):
            lanes = pl.ds(pl.multiple_of(x * wide + j * 128, 128), 128)
            out_ref[j * cols : (j + 1) * cols, :] = gate_ref[:, lanes]
    for copy in copies[:3]:
        copy.wait()
    middle = first_ref.shape[0] // 2
    top = jnp.concatenate([key_ref[...], first_ref[:middle].astype(BF16)], axis=0)
    bottom = jnp.concatenate(
        [first_ref[middle:].astype(BF16), second_ref[...].astype(BF16)], axis=0
    )
    even = jnp.full(top.shape, at_ref[3], jnp.int32) == 0
    keep_ref[...] = jnp.where(even, top, bottom)
    give_ref[...] = jnp.where(even, bottom, top)
    copies[3].wait()


def gate_kernel(
    at_ref, w0, w1, w2, w3, own_ref, other_ref, here_ref, out_hbm, out_ref, sems
):
    rows = jnp.concatenate(
        [ref[y, half] for ref in (own_ref, other_ref) for y in range(SIDE) for half in range(2)],
        axis=1,
    )
    writes = []
    for k, (step, w_ref) in enumerate(zip(GATE_ORDER, (w0, w1, w2, w3))):
        x = lax.rem(at_ref[0] + SIDE - step, SIDE)
        parts = []
        for core in (at_ref[2], 1 - at_ref[2]):
            for y in ROWS_ORDER:
                for half in range(2):
                    j = lax.rem(at_ref[1] + y, SIDE) * 4 + half * 2 + core
                    parts.append(w_ref[pl.ds(pl.multiple_of(j * 128, 128), 128), :])
        total = lax.dot_general(
            jnp.concatenate(parts, axis=1),
            rows,
            (((1,), (1,)), ((), ())),
            preferred_element_type=F32,
        )
        out_ref[k] = total.astype(BF16)
        writes.append(pltpu.make_async_copy(out_ref.at[k], out_hbm.at[x], sems.at[k]))
        writes[-1].start()
        if step == 0:
            here_ref[...] = total
    for write in writes:
        write.wait()


def down_kernel(
    at_ref, down_hbm, other_ref, hidden_ref, mine_ref, theirs_ref, own_ref, sem
):
    read = pltpu.make_async_copy(down_hbm.at[:, at_ref[2]], own_ref, sem)
    read.start()
    chips, rows, wide = hidden_ref.shape
    hidden = jnp.concatenate([hidden_ref[i] for i in range(chips)], axis=1)
    read.wait()
    lower = jnp.concatenate(
        [ref[...].reshape(chips * wide, wide) for ref in (own_ref, other_ref)], axis=1
    )
    total = jnp.dot(hidden, lower, preferred_element_type=F32)
    mine_ref[...] = total[:, :wide]
    theirs_ref[...] = total[:, wide:]


def add_back(here, got, x):
    for step in range(SIDE):
        here = here + jnp.where(x == step, 0.0, got[step].astype(F32))
    return here


def body(
    key_weights, first_moment, second_moment, tokens, routes, route_weights, gate_up, down_proj
):
    branches = lax.axis_size("b")
    half, x, core = lax.axis_index("zh"), lax.axis_index("x"), lax.axis_index("c")
    branch = lax.axis_index("b")
    low, mid = branch % 2, (branch // 2) % 2
    at = jnp.stack([x, lax.axis_index("y"), core, low]).astype(jnp.int32)
    group_rows, width = tokens.shape
    capacity = 4 * group_rows // branches
    slots = branches * capacity
    hidden_here = gate_up.shape[2]
    rows_here = key_weights.shape[1]

    slotted, pick = call(
        route_kernel,
        [
            jax.ShapeDtypeStruct((2 * slots, width), BF16),
            jax.ShapeDtypeStruct((slots, 2 * group_rows), BF16),
        ],
        at,
        in_hbm(routes.T),
        in_hbm(tokens),
        spaces=[pltpu.HBM] * 2,
        scratch=[
            pltpu.VMEM(routes.T.shape, jnp.int32),
            pltpu.VMEM(tokens.shape, BF16),
            pltpu.SemaphoreType.DMA((2,)),
        ],
    )
    arrived = exchange(slotted.reshape(2 * branches, capacity, width), ("zh", "b"))

    gate_w = gate_up[0].reshape(2 * hidden_here, -1)
    columns = key_weights.shape[2]
    cut = jax.ShapeDtypeStruct((gate_w.size // SIDE // width, width), BF16)
    part = jax.ShapeDtypeStruct((3 * rows_here // 2, columns), BF16)
    lower = down_proj[0].reshape(-1, 2, hidden_here, width)
    *cuts, keep, give, other_lower = call(
        split_kernel,
        [cut] * SIDE + [part] * 2 + [jax.ShapeDtypeStruct((lower.shape[0],) + lower.shape[2:], BF16)],
        at,
        gate_w,
        in_hbm(key_weights[0]),
        in_hbm(first_moment[0]),
        in_hbm(second_moment[0]),
        in_hbm(lower),
        spaces=[pltpu.VMEM] + [pltpu.HBM] * 4,
        scratch=[
            pltpu.VMEM((rows_here, columns), BF16),
            pltpu.VMEM((rows_here, columns), F32),
            pltpu.VMEM((rows_here, columns), F32),
            pltpu.SemaphoreType.DMA((4,)),
        ],
    )
    weights = to_peers(cuts, GATE_ORDER)
    other_lower = flip(other_lower, "c")

    rows = arrived.reshape(2, slots, width)
    line = [rows] + [shift(rows, "y", -ahead) for ahead in ROWS_ORDER[1:]]
    line, weights, give = lax.optimization_barrier((line, weights, give))
    line = jnp.stack(line)
    line_other = flip(line, "c")
    got = flip(give, "b", 1)

    cols = 2 * hidden_here
    here, others = call(
        gate_kernel,
        [jax.ShapeDtypeStruct((cols, slots), F32), pltpu.HBM((SIDE, cols, slots), BF16)],
        at,
        *weights,
        line,
        line_other,
        out_spaces=[pltpu.VMEM, pltpu.HBM],
        scratch=[pltpu.VMEM((SIDE, cols, slots), BF16), pltpu.SemaphoreType.DMA((SIDE,))],
    )
    others, keep, got = lax.optimization_barrier((others, keep, got))
    slabs = (keep.astype(F32) + got.astype(F32)).reshape(2, -1, columns)
    give = lax.dynamic_index_in_dim(slabs, 1 - mid, 0, keepdims=False).astype(BF16)
    keep = lax.dynamic_index_in_dim(slabs, mid, 0, keepdims=False).astype(BF16)
    got = flip(give, "b", 2)
    gated = add_back(here, exchange(others, "x"), x)
    hidden = (jax.nn.silu(gated[:hidden_here]) * gated[hidden_here:]).astype(BF16)

    swap = flip(hidden, "zh")
    swap, got = lax.optimization_barrier((swap, got))

    both = jnp.where(
        half == 0,
        jnp.concatenate([hidden, swap], axis=0),
        jnp.concatenate([swap, hidden], axis=0),
    )
    spread = gather(both.T, ("x", "y"))
    slabs = (keep.astype(F32) + got.astype(F32)).astype(BF16)
    got = flip(slabs, "b", 4)
    slabs = ((slabs.astype(F32) + got.astype(F32)) / branches).astype(BF16)
    got = flip(slabs, "b", 2)
    spread, slabs, got = lax.optimization_barrier((spread, slabs, got))

    mine, theirs = call(
        down_kernel,
        [jax.ShapeDtypeStruct((slots, width), F32)] * 2,
        at,
        in_hbm(lower),
        other_lower,
        spread,
        spaces=[pltpu.HBM] + [pltpu.VMEM] * 2,
        scratch=[pltpu.VMEM(other_lower.shape, BF16), pltpu.SemaphoreType.DMA],
    )
    out = (mine + flip(theirs, "c")).astype(BF16)
    out, slabs, got = lax.optimization_barrier((out, slabs, got))
    slabs = jnp.stack([jnp.where(mid == 0, slabs, got), jnp.where(mid == 0, got, slabs)])
    got = flip(slabs, "b", 1)
    back = exchange(out.reshape(branches, capacity, width), "b").reshape(slots, width)
    back, got = lax.optimization_barrier((back, got))
    slabs = jnp.stack([jnp.where(low == 0, slabs, got), jnp.where(low == 0, got, slabs)])
    slabs = slabs.reshape(3 * rows_here, -1)
    picked = lax.dot_general(
        pick, back, (((0,), (0,)), ((), ())), preferred_element_type=F32
    )
    mixed = (
        route_weights[:, 0:1] * picked[:group_rows] + route_weights[:, 1:2] * picked[group_rows:]
    ).astype(BF16)
    return (
        slabs[:rows_here],
        slabs[rows_here : 2 * rows_here].astype(F32),
        slabs[2 * rows_here :].astype(F32),
        mixed,
    )


def solution(mesh):
    fine = Mesh(mesh.devices.reshape(8, SIDE, SIDE, 2, 2), ("b",) + SHARD)
    return jax.shard_map(
        body,
        mesh=fine,
        in_specs=(
            P("b", SHARD, None),
            P("b", SHARD, None),
            P("b", SHARD, None),
            P("b", SHARD),
            P("b", None),
            P("b", None),
            P("b", None, SHARD, None),
            P("b", None, SHARD),
        ),
        out_specs=(P(SHARD, None), P(SHARD, None), P(SHARD, None), P("b", SHARD)),
        check_vma=False,
    )
```

```python
import jax
import jax.numpy as jnp
from jax import lax
from jax.experimental import pallas as pl
from jax.experimental.pallas import tpu as pltpu
from jax.sharding import Mesh
from jax.sharding import PartitionSpec as P

SIDE = 4
GATE_ORDER = (0, 1, 3, 2)
ROWS_ORDER = (0, 1, 2, 3)
VMEM = 24 * 1024 * 1024
BF16, F32 = jnp.bfloat16, jnp.float32
SHARD = ("x", "y", "zh", "c")


def shift(array, axis, step):
    size = lax.axis_size(axis)
    return lax.ppermute(array, axis, [(i, (i + step) % size) for i in range(size)])


def flip(array, axis, bit=1):
    return lax.ppermute(array, axis, [(i, i ^ bit) for i in range(lax.axis_size(axis))])


def exchange(blocks, axis):
    return lax.all_to_all(blocks, axis, split_axis=0, concat_axis=0, tiled=True)


def gather(block, axis):
    size = lax.axis_size(axis)
    return exchange(jnp.broadcast_to(block[None], (size,) + block.shape), axis)


def to_peers(cuts, order):
    return [shift(cuts[step], "x", step) if step else cuts[step] for step in order]


def in_hbm(array):
    return pltpu.with_memory_space_constraint(array, pltpu.HBM)


def call(kernel, out_shape, at, *arrays, spaces=None, out_spaces=None, scratch=()):
    spaces = spaces or [pltpu.VMEM] * len(arrays)
    out_spaces = out_spaces or [pltpu.VMEM] * len(out_shape)
    return pl.pallas_call(
        kernel,
        out_shape=out_shape,
        in_specs=[pl.BlockSpec(memory_space=space) for space in [pltpu.SMEM] + list(spaces)],
        out_specs=[pl.BlockSpec(memory_space=space) for space in out_spaces],
        scratch_shapes=list(scratch),
        compiler_params=pltpu.CompilerParams(vmem_limit_bytes=VMEM),
    )(at, *arrays)


def route_kernel(
    at_ref, routes_hbm, tokens_hbm, slotted_ref, pick_ref, routes_ref, tokens_ref, sems
):
    reads = [
        pltpu.make_async_copy(routes_hbm, routes_ref, sems.at[0]),
        pltpu.make_async_copy(tokens_hbm, tokens_ref, sems.at[1]),
    ]
    for read in reads:
        read.start()
    for read in reads:
        read.wait()
    rows = tokens_ref.shape[0]
    slots = slotted_ref.shape[0] // 2
    experts = 8
    capacity = slots // experts
    label = lax.broadcasted_iota(jnp.int32, (experts, rows), 0)
    first = (routes_ref[0:1, :] == label).astype(F32)
    second = (routes_ref[1:2, :] == label).astype(F32)
    named = first + second
    earlier = (
        lax.broadcasted_iota(jnp.int32, (rows, rows), 0)
        < lax.broadcasted_iota(jnp.int32, (rows, rows), 1)
    ).astype(F32)
    before = jnp.dot(named, earlier, preferred_element_type=F32).astype(jnp.int32)
    position = lax.broadcasted_iota(jnp.int32, (capacity, rows), 0)
    members = []
    for e in range(experts):
        hit = (before[e : e + 1] == position).astype(F32)
        span = slice(e * capacity, (e + 1) * capacity)
        pick_ref[span, :rows] = (hit * first[e : e + 1]).astype(BF16)
        pick_ref[span, rows:] = (hit * second[e : e + 1]).astype(BF16)
        members.append((hit * named[e : e + 1]).astype(BF16))
    slotted = jnp.dot(
        jnp.concatenate(members, axis=0), tokens_ref[...], preferred_element_type=F32
    ).astype(BF16)
    slotted_ref[:slots] = slotted
    slotted_ref[slots:] = slotted


def split_kernel(
    at_ref, gate_hbm, key_hbm, first_hbm, second_hbm, down_hbm,
    c0, c1, c2, c3, keep_ref, give_ref, lower_ref,
    gate_ref, key_ref, first_ref, second_ref, gate_sems, sems,
):
    wide, cols = gate_ref.shape[2], gate_ref.shape[1]
    reads = []
    for step in range(SIDE):
        lanes = pl.ds(pl.multiple_of(lax.rem(at_ref[0] + step, SIDE) * wide, wide), wide)
        reads.append(
            pltpu.make_async_copy(gate_hbm.at[:, lanes], gate_ref.at[step], gate_sems.at[step])
        )
    copies = [
        pltpu.make_async_copy(source, target, sems.at[i])
        for i, (source, target) in enumerate(
            (
                (key_hbm, key_ref),
                (first_hbm, first_ref),
                (second_hbm, second_ref),
                (down_hbm.at[:, 1 - at_ref[2]], lower_ref),
            )
        )
    ]
    for copy in reads + copies:
        copy.start()
    for step, out_ref in enumerate((c0, c1, c2, c3)):
        reads[step].wait()
        for j in range(wide // 128):
            lanes = slice(j * 128, (j + 1) * 128)
            out_ref[j * cols : (j + 1) * cols, :] = gate_ref[step, :, lanes]
    for copy in copies[:3]:
        copy.wait()
    middle = first_ref.shape[0] // 2
    top = jnp.concatenate([key_ref[...], first_ref[:middle].astype(BF16)], axis=0)
    bottom = jnp.concatenate(
        [first_ref[middle:].astype(BF16), second_ref[...].astype(BF16)], axis=0
    )
    even = jnp.full(top.shape, at_ref[3], jnp.int32) == 0
    keep_ref[...] = jnp.where(even, top, bottom)
    give_ref[...] = jnp.where(even, bottom, top)
    copies[3].wait()


def gate_kernel(
    at_ref, w0, w1, w2, w3, own_ref, other_ref, here_ref, out_hbm, out_ref, sems
):
    rows = jnp.concatenate(
        [ref[y, half] for ref in (own_ref, other_ref) for y in range(SIDE) for half in range(2)],
        axis=1,
    )
    writes = []
    for k, (step, w_ref) in enumerate(zip(GATE_ORDER, (w0, w1, w2, w3))):
        x = lax.rem(at_ref[0] + SIDE - step, SIDE)
        parts = []
        for core in (at_ref[2], 1 - at_ref[2]):
            for y in ROWS_ORDER:
                for half in range(2):
                    j = lax.rem(at_ref[1] + y, SIDE) * 4 + half * 2 + core
                    parts.append(w_ref[pl.ds(pl.multiple_of(j * 128, 128), 128), :])
        total = lax.dot_general(
            jnp.concatenate(parts, axis=1),
            rows,
            (((1,), (1,)), ((), ())),
            preferred_element_type=F32,
        )
        out_ref[k] = total.astype(BF16)
        writes.append(pltpu.make_async_copy(out_ref.at[k], out_hbm.at[x], sems.at[k]))
        writes[-1].start()
        if step == 0:
            here_ref[...] = total
    for write in writes:
        write.wait()


def down_kernel(
    at_ref, down_hbm, other_ref, hidden_ref, mine_ref, theirs_ref, own_ref, sem
):
    read = pltpu.make_async_copy(down_hbm.at[:, at_ref[2]], own_ref, sem)
    read.start()
    chips, rows, wide = hidden_ref.shape
    hidden = jnp.concatenate([hidden_ref[i] for i in range(chips)], axis=1)
    read.wait()
    lower = jnp.concatenate(
        [ref[...].reshape(chips * wide, wide) for ref in (own_ref, other_ref)], axis=1
    )
    total = jnp.dot(hidden, lower, preferred_element_type=F32)
    mine_ref[...] = total[:, :wide]
    theirs_ref[...] = total[:, wide:]


def add_back(here, got, x):
    for step in range(SIDE):
        here = here + jnp.where(x == step, 0.0, got[step].astype(F32))
    return here


def body(
    key_weights, first_moment, second_moment, tokens, routes, route_weights, gate_up, down_proj
):
    branches = lax.axis_size("b")
    half, x, core = lax.axis_index("zh"), lax.axis_index("x"), lax.axis_index("c")
    branch = lax.axis_index("b")
    low, mid = branch % 2, (branch // 2) % 2
    at = jnp.stack([x, lax.axis_index("y"), core, low]).astype(jnp.int32)
    group_rows, width = tokens.shape
    capacity = 4 * group_rows // branches
    slots = branches * capacity
    hidden_here = gate_up.shape[2]
    rows_here = key_weights.shape[1]

    slotted, pick = call(
        route_kernel,
        [
            jax.ShapeDtypeStruct((2 * slots, width), BF16),
            jax.ShapeDtypeStruct((slots, 2 * group_rows), BF16),
        ],
        at,
        in_hbm(routes.T),
        in_hbm(tokens),
        spaces=[pltpu.HBM] * 2,
        scratch=[
            pltpu.VMEM(routes.T.shape, jnp.int32),
            pltpu.VMEM(tokens.shape, BF16),
            pltpu.SemaphoreType.DMA((2,)),
        ],
    )
    arrived = exchange(slotted.reshape(2 * branches, capacity, width), ("zh", "b"))

    gate_w = gate_up[0].reshape(2 * hidden_here, -1)
    columns = key_weights.shape[2]
    cut = jax.ShapeDtypeStruct((gate_w.size // SIDE // width, width), BF16)
    part = jax.ShapeDtypeStruct((3 * rows_here // 2, columns), BF16)
    lower = down_proj[0].reshape(-1, 2, hidden_here, width)
    *cuts, keep, give, other_lower = call(
        split_kernel,
        [cut] * SIDE + [part] * 2 + [jax.ShapeDtypeStruct((lower.shape[0],) + lower.shape[2:], BF16)],
        at,
        in_hbm(gate_w),
        in_hbm(key_weights[0]),
        in_hbm(first_moment[0]),
        in_hbm(second_moment[0]),
        in_hbm(lower),
        spaces=[pltpu.HBM] * 5,
        scratch=[
            pltpu.VMEM((SIDE, gate_w.shape[0], gate_w.shape[1] // SIDE), BF16),
            pltpu.VMEM((rows_here, columns), BF16),
            pltpu.VMEM((rows_here, columns), F32),
            pltpu.VMEM((rows_here, columns), F32),
            pltpu.SemaphoreType.DMA((SIDE,)),
            pltpu.SemaphoreType.DMA((4,)),
        ],
    )
    weights = to_peers(cuts, GATE_ORDER)
    got = flip(give, "b", 1)
    other_lower = flip(other_lower, "c")

    arrived, other_lower = lax.optimization_barrier((arrived, other_lower))
    rows = arrived.reshape(2, slots, width)
    line = [rows] + [shift(rows, "y", -ahead) for ahead in ROWS_ORDER[1:]]
    line, weights, got = lax.optimization_barrier((line, weights, got))
    line = jnp.stack(line)
    line_other = flip(line, "c")

    cols = 2 * hidden_here
    here, others = call(
        gate_kernel,
        [jax.ShapeDtypeStruct((cols, slots), F32), pltpu.HBM((SIDE, cols, slots), BF16)],
        at,
        *weights,
        line,
        line_other,
        out_spaces=[pltpu.VMEM, pltpu.HBM],
        scratch=[pltpu.VMEM((SIDE, cols, slots), BF16), pltpu.SemaphoreType.DMA((SIDE,))],
    )
    others, keep, got = lax.optimization_barrier((others, keep, got))
    slabs = (keep.astype(F32) + got.astype(F32)).reshape(2, -1, columns)
    give = lax.dynamic_index_in_dim(slabs, 1 - mid, 0, keepdims=False).astype(BF16)
    keep = lax.dynamic_index_in_dim(slabs, mid, 0, keepdims=False).astype(BF16)
    got = flip(give, "b", 2)
    gated = add_back(here, exchange(others, "x"), x)
    hidden = (jax.nn.silu(gated[:hidden_here]) * gated[hidden_here:]).astype(BF16)

    swap = flip(hidden, "zh")
    slabs = (keep.astype(F32) + got.astype(F32)).astype(BF16)
    swap, slabs = lax.optimization_barrier((swap, slabs))

    both = jnp.where(
        half == 0,
        jnp.concatenate([hidden, swap], axis=0),
        jnp.concatenate([swap, hidden], axis=0),
    )
    spread = gather(both.T, ("x", "y"))
    got = flip(slabs, "b", 4)
    slabs = ((slabs.astype(F32) + got.astype(F32)) / branches).astype(BF16)
    got = flip(slabs, "b", 2)
    spread, slabs, got = lax.optimization_barrier((spread, slabs, got))

    mine, theirs = call(
        down_kernel,
        [jax.ShapeDtypeStruct((slots, width), F32)] * 2,
        at,
        in_hbm(lower),
        other_lower,
        spread,
        spaces=[pltpu.HBM] + [pltpu.VMEM] * 2,
        scratch=[pltpu.VMEM(other_lower.shape, BF16), pltpu.SemaphoreType.DMA],
    )
    out = (mine + flip(theirs, "c")).astype(BF16)
    out, slabs, got = lax.optimization_barrier((out, slabs, got))
    slabs = jnp.stack([jnp.where(mid == 0, slabs, got), jnp.where(mid == 0, got, slabs)])
    got = flip(slabs, "b", 1)
    back = exchange(out.reshape(branches, capacity, width), "b").reshape(slots, width)
    back, got = lax.optimization_barrier((back, got))
    slabs = jnp.stack([jnp.where(low == 0, slabs, got), jnp.where(low == 0, got, slabs)])
    slabs = slabs.reshape(3 * rows_here, -1)
    picked = lax.dot_general(
        pick, back, (((0,), (0,)), ((), ())), preferred_element_type=F32
    )
    mixed = (
        route_weights[:, 0:1] * picked[:group_rows] + route_weights[:, 1:2] * picked[group_rows:]
    ).astype(BF16)
    return (
        slabs[:rows_here],
        slabs[rows_here : 2 * rows_here].astype(F32),
        slabs[2 * rows_here :].astype(F32),
        mixed,
    )


def solution(mesh):
    fine = Mesh(mesh.devices.reshape(8, SIDE, SIDE, 2, 2), ("b",) + SHARD)
    return jax.shard_map(
        body,
        mesh=fine,
        in_specs=(
            P("b", SHARD, None),
            P("b", SHARD, None),
            P("b", SHARD, None),
            P("b", SHARD),
            P("b", None),
            P("b", None),
            P("b", None, SHARD, None),
            P("b", None, SHARD),
        ),
        out_specs=(P(SHARD, None), P(SHARD, None), P(SHARD, None), P("b", SHARD)),
        check_vma=False,
    )
```

```python
import jax
import jax.numpy as jnp
from jax import lax
from jax.experimental import pallas as pl
from jax.experimental.pallas import tpu as pltpu
from jax.sharding import Mesh
from jax.sharding import PartitionSpec as P

SIDE = 4
GATE_ORDER = (0, 1, 3, 2)
ROWS_ORDER = (0, 1, 2, 3)
VMEM = 24 * 1024 * 1024
BF16, F32 = jnp.bfloat16, jnp.float32
SHARD = ("x", "y", "zh", "c")


def shift(array, axis, step):
    size = lax.axis_size(axis)
    return lax.ppermute(array, axis, [(i, (i + step) % size) for i in range(size)])


def flip(array, axis, bit=1):
    return lax.ppermute(array, axis, [(i, i ^ bit) for i in range(lax.axis_size(axis))])


def exchange(blocks, axis):
    return lax.all_to_all(blocks, axis, split_axis=0, concat_axis=0, tiled=True)


def gather(block, axis):
    size = lax.axis_size(axis)
    return exchange(jnp.broadcast_to(block[None], (size,) + block.shape), axis)


def to_peers(cuts, order):
    return [shift(cuts[step], "x", step) if step else cuts[step] for step in order]


def in_hbm(array):
    return pltpu.with_memory_space_constraint(array, pltpu.HBM)


def call(kernel, out_shape, at, *arrays, spaces=None, out_spaces=None, scratch=()):
    spaces = spaces or [pltpu.VMEM] * len(arrays)
    out_spaces = out_spaces or [pltpu.VMEM] * len(out_shape)
    return pl.pallas_call(
        kernel,
        out_shape=out_shape,
        in_specs=[pl.BlockSpec(memory_space=space) for space in [pltpu.SMEM] + list(spaces)],
        out_specs=[pl.BlockSpec(memory_space=space) for space in out_spaces],
        scratch_shapes=list(scratch),
        compiler_params=pltpu.CompilerParams(vmem_limit_bytes=VMEM),
    )(at, *arrays)


def route_kernel(
    at_ref, routes_hbm, tokens_hbm, slotted_ref, pick_ref, routes_ref, tokens_ref, sems
):
    reads = [
        pltpu.make_async_copy(routes_hbm, routes_ref, sems.at[0]),
        pltpu.make_async_copy(tokens_hbm, tokens_ref, sems.at[1]),
    ]
    for read in reads:
        read.start()
    for read in reads:
        read.wait()
    rows = tokens_ref.shape[0]
    slots = slotted_ref.shape[0] // 2
    experts = 8
    capacity = slots // experts
    label = lax.broadcasted_iota(jnp.int32, (experts, rows), 0)
    first = (routes_ref[0:1, :] == label).astype(F32)
    second = (routes_ref[1:2, :] == label).astype(F32)
    named = first + second
    earlier = (
        lax.broadcasted_iota(jnp.int32, (rows, rows), 0)
        < lax.broadcasted_iota(jnp.int32, (rows, rows), 1)
    ).astype(F32)
    before = jnp.dot(named, earlier, preferred_element_type=F32).astype(jnp.int32)
    position = lax.broadcasted_iota(jnp.int32, (capacity, rows), 0)
    members = []
    for e in range(experts):
        hit = (before[e : e + 1] == position).astype(F32)
        span = slice(e * capacity, (e + 1) * capacity)
        pick_ref[span, :rows] = (hit * first[e : e + 1]).astype(BF16)
        pick_ref[span, rows:] = (hit * second[e : e + 1]).astype(BF16)
        members.append((hit * named[e : e + 1]).astype(BF16))
    slotted = jnp.dot(
        jnp.concatenate(members, axis=0), tokens_ref[...], preferred_element_type=F32
    ).astype(BF16)
    slotted_ref[:slots] = slotted
    slotted_ref[slots:] = slotted


def split_kernel(
    at_ref, gate_hbm, key_hbm, first_hbm, second_hbm, down_hbm,
    c0, c1, c2, c3, keep_ref, give_ref, lower_ref,
    gate_ref, key_ref, first_ref, second_ref, gate_sems, sems,
):
    wide, cols = gate_ref.shape[2], gate_ref.shape[1]
    reads = []
    for step in range(SIDE):
        lanes = pl.ds(pl.multiple_of(lax.rem(at_ref[0] + step, SIDE) * wide, wide), wide)
        reads.append(
            pltpu.make_async_copy(gate_hbm.at[:, lanes], gate_ref.at[step], gate_sems.at[step])
        )
    copies = [
        pltpu.make_async_copy(source, target, sems.at[i])
        for i, (source, target) in enumerate(
            (
                (key_hbm, key_ref),
                (first_hbm, first_ref),
                (second_hbm, second_ref),
                (down_hbm.at[:, 1 - at_ref[2]], lower_ref),
            )
        )
    ]
    for copy in reads + copies:
        copy.start()
    for step, out_ref in enumerate((c0, c1, c2, c3)):
        reads[step].wait()
        for j in range(wide // 128):
            lanes = slice(j * 128, (j + 1) * 128)
            out_ref[j * cols : (j + 1) * cols, :] = gate_ref[step, :, lanes]
    for copy in copies[:3]:
        copy.wait()
    middle = first_ref.shape[0] // 2
    top = jnp.concatenate([key_ref[...], first_ref[:middle].astype(BF16)], axis=0)
    bottom = jnp.concatenate(
        [first_ref[middle:].astype(BF16), second_ref[...].astype(BF16)], axis=0
    )
    even = jnp.full(top.shape, at_ref[3], jnp.int32) == 0
    keep_ref[...] = jnp.where(even, top, bottom)
    give_ref[...] = jnp.where(even, bottom, top)
    copies[3].wait()


def gate_kernel(
    at_ref, w0, w1, w2, w3, own_ref, other_ref, here_ref, out_hbm, out_ref, sems
):
    rows = jnp.concatenate(
        [ref[y, half] for ref in (own_ref, other_ref) for y in range(SIDE) for half in range(2)],
        axis=1,
    )
    writes = []
    for k, (step, w_ref) in enumerate(zip(GATE_ORDER, (w0, w1, w2, w3))):
        x = lax.rem(at_ref[0] + SIDE - step, SIDE)
        parts = []
        for core in (at_ref[2], 1 - at_ref[2]):
            for y in ROWS_ORDER:
                for half in range(2):
                    j = lax.rem(at_ref[1] + y, SIDE) * 4 + half * 2 + core
                    parts.append(w_ref[pl.ds(pl.multiple_of(j * 128, 128), 128), :])
        total = lax.dot_general(
            jnp.concatenate(parts, axis=1),
            rows,
            (((1,), (1,)), ((), ())),
            preferred_element_type=F32,
        )
        out_ref[k] = total.astype(BF16)
        writes.append(pltpu.make_async_copy(out_ref.at[k], out_hbm.at[x], sems.at[k]))
        writes[-1].start()
        if step == 0:
            here_ref[...] = total
    for write in writes:
        write.wait()


def down_kernel(
    at_ref, down_hbm, other_ref, hidden_ref, mine_ref, theirs_ref, own_ref, sem
):
    read = pltpu.make_async_copy(down_hbm.at[:, at_ref[2]], own_ref, sem)
    read.start()
    chips, rows, wide = hidden_ref.shape
    hidden = jnp.concatenate([hidden_ref[i] for i in range(chips)], axis=1)
    read.wait()
    lower = jnp.concatenate(
        [ref[...].reshape(chips * wide, wide) for ref in (own_ref, other_ref)], axis=1
    )
    total = jnp.dot(hidden, lower, preferred_element_type=F32)
    mine_ref[...] = total[:, :wide]
    theirs_ref[...] = total[:, wide:]


def add_back(here, got, x):
    for step in range(SIDE):
        here = here + jnp.where(x == step, 0.0, got[step].astype(F32))
    return here


def body(
    key_weights, first_moment, second_moment, tokens, routes, route_weights, gate_up, down_proj
):
    branches = lax.axis_size("b")
    half, x, core = lax.axis_index("zh"), lax.axis_index("x"), lax.axis_index("c")
    branch = lax.axis_index("b")
    low, mid = branch % 2, (branch // 2) % 2
    at = jnp.stack([x, lax.axis_index("y"), core, low]).astype(jnp.int32)
    group_rows, width = tokens.shape
    capacity = 4 * group_rows // branches
    slots = branches * capacity
    hidden_here = gate_up.shape[2]
    rows_here = key_weights.shape[1]

    slotted, pick = call(
        route_kernel,
        [
            jax.ShapeDtypeStruct((2 * slots, width), BF16),
            jax.ShapeDtypeStruct((slots, 2 * group_rows), BF16),
        ],
        at,
        in_hbm(routes.T),
        in_hbm(tokens),
        spaces=[pltpu.HBM] * 2,
        scratch=[
            pltpu.VMEM(routes.T.shape, jnp.int32),
            pltpu.VMEM(tokens.shape, BF16),
            pltpu.SemaphoreType.DMA((2,)),
        ],
    )
    arrived = exchange(slotted.reshape(2 * branches, capacity, width), ("zh", "b"))

    gate_w = gate_up[0].reshape(2 * hidden_here, -1)
    columns = key_weights.shape[2]
    cut = jax.ShapeDtypeStruct((gate_w.size // SIDE // width, width), BF16)
    part = jax.ShapeDtypeStruct((3 * rows_here // 2, columns), BF16)
    lower = down_proj[0].reshape(-1, 2, hidden_here, width)
    *cuts, keep, give, other_lower = call(
        split_kernel,
        [cut] * SIDE + [part] * 2 + [jax.ShapeDtypeStruct((lower.shape[0],) + lower.shape[2:], BF16)],
        at,
        in_hbm(gate_w),
        in_hbm(key_weights[0]),
        in_hbm(first_moment[0]),
        in_hbm(second_moment[0]),
        in_hbm(lower),
        spaces=[pltpu.HBM] * 5,
        scratch=[
            pltpu.VMEM((SIDE, gate_w.shape[0], gate_w.shape[1] // SIDE), BF16),
            pltpu.VMEM((rows_here, columns), BF16),
            pltpu.VMEM((rows_here, columns), F32),
            pltpu.VMEM((rows_here, columns), F32),
            pltpu.SemaphoreType.DMA((SIDE,)),
            pltpu.SemaphoreType.DMA((4,)),
        ],
    )
    weights = to_peers(cuts, GATE_ORDER)
    other_lower = flip(other_lower, "c")

    rows = arrived.reshape(2, slots, width)
    line = [rows] + [shift(rows, "y", -ahead) for ahead in ROWS_ORDER[1:]]
    line, weights, give = lax.optimization_barrier((line, weights, give))
    line = jnp.stack(line)
    line_other = flip(line, "c")
    got = flip(give, "b", 1)

    cols = 2 * hidden_here
    here, others = call(
        gate_kernel,
        [jax.ShapeDtypeStruct((cols, slots), F32), pltpu.HBM((SIDE, cols, slots), BF16)],
        at,
        *weights,
        line,
        line_other,
        out_spaces=[pltpu.VMEM, pltpu.HBM],
        scratch=[pltpu.VMEM((SIDE, cols, slots), BF16), pltpu.SemaphoreType.DMA((SIDE,))],
    )
    others, keep, got = lax.optimization_barrier((others, keep, got))
    slabs = (keep.astype(F32) + got.astype(F32)).reshape(2, -1, columns)
    give = lax.dynamic_index_in_dim(slabs, 1 - mid, 0, keepdims=False).astype(BF16)
    keep = lax.dynamic_index_in_dim(slabs, mid, 0, keepdims=False).astype(BF16)
    got = flip(give, "b", 2)
    gated = add_back(here, exchange(others, "x"), x)
    hidden = (jax.nn.silu(gated[:hidden_here]) * gated[hidden_here:]).astype(BF16)

    swap = flip(hidden, "zh")
    swap, got = lax.optimization_barrier((swap, got))

    both = jnp.where(
        half == 0,
        jnp.concatenate([hidden, swap], axis=0),
        jnp.concatenate([swap, hidden], axis=0),
    )
    spread = gather(both.T, ("x", "y"))
    slabs = (keep.astype(F32) + got.astype(F32)).astype(BF16)
    got = flip(slabs, "b", 4)
    slabs = ((slabs.astype(F32) + got.astype(F32)) / branches).astype(BF16)
    got = flip(slabs, "b", 2)
    spread, slabs, got = lax.optimization_barrier((spread, slabs, got))

    mine, theirs = call(
        down_kernel,
        [jax.ShapeDtypeStruct((slots, width), F32)] * 2,
        at,
        in_hbm(lower),
        other_lower,
        spread,
        spaces=[pltpu.HBM] + [pltpu.VMEM] * 2,
        scratch=[pltpu.VMEM(other_lower.shape, BF16), pltpu.SemaphoreType.DMA],
    )
    out = (mine + flip(theirs, "c")).astype(BF16)
    out, slabs, got = lax.optimization_barrier((out, slabs, got))
    slabs = jnp.stack([jnp.where(mid == 0, slabs, got), jnp.where(mid == 0, got, slabs)])
    got = flip(slabs, "b", 1)
    back = exchange(out.reshape(branches, capacity, width), "b").reshape(slots, width)
    back, got = lax.optimization_barrier((back, got))
    slabs = jnp.stack([jnp.where(low == 0, slabs, got), jnp.where(low == 0, got, slabs)])
    slabs = slabs.reshape(3 * rows_here, -1)
    picked = lax.dot_general(
        pick, back, (((0,), (0,)), ((), ())), preferred_element_type=F32
    )
    mixed = (
        route_weights[:, 0:1] * picked[:group_rows] + route_weights[:, 1:2] * picked[group_rows:]
    ).astype(BF16)
    return (
        slabs[:rows_here],
        slabs[rows_here : 2 * rows_here].astype(F32),
        slabs[2 * rows_here :].astype(F32),
        mixed,
    )


def solution(mesh):
    fine = Mesh(mesh.devices.reshape(8, SIDE, SIDE, 2, 2), ("b",) + SHARD)
    return jax.shard_map(
        body,
        mesh=fine,
        in_specs=(
            P("b", SHARD, None),
            P("b", SHARD, None),
            P("b", SHARD, None),
            P("b", SHARD),
            P("b", None),
            P("b", None),
            P("b", None, SHARD, None),
            P("b", None, SHARD),
        ),
        out_specs=(P(SHARD, None), P(SHARD, None), P(SHARD, None), P("b", SHARD)),
        check_vma=False,
    )
```
